256 devices in a mesh: dp: 8 (over z), expert: 2 (over core), tensor: 16 (over y, x).
Axes of the slice: x: 4, y: 4, z: 8, core: 2. Of those that a mesh axis runs over, the one named last changes fastest.
Arguments:
- tokens: bfloat16 [8192, 6144], P(('dp', 'expert'), 'tensor'), parts along dimension 0, may hold values from -6 to 6
- route_ids: int32 [8192, 2], P(('dp', 'expert')), parts along dimension 0, may hold values from 0 to 7, as said below
- route_gates: float32 [8192, 2], P(('dp', 'expert')), parts along dimension 0, may hold values from 0.2 to 1
- w_gate: bfloat16 [2, 6144, 8192], P('expert', None, 'tensor'), may hold values from -0.078125 to 0.078125
- w_up: bfloat16 [2, 6144, 8192], P('expert', None, 'tensor'), may hold values from -0.078125 to 0.078125
- w_down: bfloat16 [2, 8192, 6144], P('expert', 'tensor'), may hold values from -0.0625 to 0.0625
Outputs:
- mixed: bfloat16 [8192, 6144], P(('dp', 'expert'), 'tensor'), parts along dimension 0
The draws below stay inside these ranges and needn't reach their ends.
There are 8 independent parts, one for each index of `dp`. The reference program is written for one: setup_inputs(seed, part) draws one part's arguments, and reference() takes and returns one part's arrays. A program takes and returns all parts, laid end to end along the dimension named above; an argument that names none is the same for every part. Nothing has to cross between parts.
Inputs may be any that keep to these rules, and one draw needn't show every extreme that they name: `route_ids`: in each aligned block of 512 rows (the rows of one expert index) every expert is named at most 256 times, and one expert below 2, the same in all blocks of a replica, is named exactly 256 times in every block. The 2 experts of a row differ.
All inputs are finite; a program needn't handle non-finite values.
Results may differ from the reference program's by a relative error of at most 0.0057.
Values may be sent and summed in bfloat16 or wider, within the bound.
No kernel may reach another device: no remote copies, remote signals or barrier semaphores. Data moves between devices by JAX's collectives and lax.ppermute only.
A program may use at most 128 MiB of HBM per device.

```python
import jax
import jax.numpy as jnp
from jax import lax

D = 6144
ROUTED = 8
TOP = 2
TOK_DEV = 512
EXPERTS = 2
FF = 8192
TOKENS = 1024
CAP = 256


def shuffle_rows(key_one):
    return jax.random.permutation(key_one, TOK_DEV)


def draw_route_ids(key, part):
    key = jax.random.fold_in(key, 11)
    key_full, key_weights, key_order, key_swap = jax.random.split(key, 4)
    blocks = TOKENS // TOK_DEV
    others = ROUTED - 1
    remain = TOP * TOK_DEV - CAP
    full = jax.random.randint(key_full, (), 0, EXPERTS)
    weights = jax.random.randint(key_weights, (blocks, others), 2, 6)
    shares = remain * weights // jnp.sum(weights, axis=1, keepdims=True)
    shortfall = remain - jnp.sum(shares, axis=1, keepdims=True)
    shares = shares + (jnp.arange(others, dtype=jnp.int32)[None, :] < shortfall).astype(jnp.int32)
    expert_ids = jnp.arange(ROUTED, dtype=jnp.int32)
    other_index = expert_ids - (expert_ids > full).astype(jnp.int32)
    other_index = jnp.clip(other_index, 0, others - 1)
    counts = jnp.where(expert_ids[None, :] == full, CAP, jnp.take(shares, other_index, axis=1))
    ends = jnp.cumsum(counts, axis=1)
    slot_ids = jnp.arange(TOP * TOK_DEV, dtype=jnp.int32)
    labels = jnp.sum((ends[:, None, :] <= slot_ids[None, :, None]).astype(jnp.int32), axis=2)
    pairs = jnp.stack([labels[:, :TOK_DEV], labels[:, TOK_DEV:]], axis=2)
    orders = jax.vmap(shuffle_rows)(jax.random.split(key_order, blocks))
    pairs = jnp.take_along_axis(pairs, orders[:, :, None], axis=1)
    swapped = jax.random.randint(key_swap, (blocks, TOK_DEV, 1), 0, 2)
    pairs = jnp.where(swapped == 1, pairs[:, :, ::-1], pairs)
    return pairs.reshape(TOKENS, TOP).astype(jnp.int32)


def block_levels(key, shape, cuts, smallest, high):
    gain = 1.0
    for dim, parts in cuts:
        heights = jax.random.uniform(jax.random.fold_in(jax.random.fold_in(key, 6), dim), (parts,), jnp.float32, smallest / len(cuts), high / len(cuts))
        gain = gain * jnp.repeat(jnp.exp(heights), shape[dim] // parts).reshape((-1,) + (1,) * (len(shape) - 1 - dim))
    return gain


def gaussian(own_key, extent, scale, most, shards=(), kind=jnp.bfloat16):
    gain = block_levels(own_key, extent, shards, -0.22, 0.18) if shards else 1.0
    values = jax.random.normal(own_key, extent, jnp.float32) * scale * gain
    return jnp.minimum(jnp.maximum(values, -most), most).astype(kind)


def setup_inputs(seed: int = 0, part: int = 0) -> dict:
    key_list = jax.random.split(jax.random.key(seed), 7)
    part_keys = jax.random.split(jax.random.fold_in(key_list[6], part), 7)
    return {
        "tokens": gaussian(part_keys[0], (TOKENS, D), 1.0, 6.0, ((0, 2), (1, 16))),
        "route_ids": draw_route_ids(jax.random.fold_in(jax.random.fold_in(key_list[6], part), 71), part),
        "route_gates": jnp.clip(0.2 + 0.8 * jax.random.uniform(part_keys[2], (TOKENS, TOP), jnp.float32) ** block_levels(part_keys[2], (TOKENS, TOP), ((0, 2),), -0.2, 0.2), 0.2, 1.0),
        "w_gate": gaussian(key_list[3], (EXPERTS, D, FF), D ** -0.5, 0.078125, ((0, 2), (2, 16))),
        "w_up": gaussian(key_list[4], (EXPERTS, D, FF), D ** -0.5, 0.078125, ((0, 2), (2, 16))),
        "w_down": gaussian(key_list[5], (EXPERTS, FF, D), FF ** -0.5, 0.0625, ((0, 2), (1, 16))),
    }


def reference(tokens, route_ids, route_gates, w_gate, w_up, w_down):
    def one_expert(total, index):
        weight = jnp.sum(jnp.where(route_ids == index, route_gates, 0.0), axis=1)
        gate = jnp.dot(tokens, w_gate[index], preferred_element_type=jnp.float32)
        upper = jnp.dot(tokens, w_up[index], preferred_element_type=jnp.float32)
        gated = (jax.nn.silu(gate) * upper).astype(jnp.bfloat16)
        result = jnp.dot(gated, w_down[index], preferred_element_type=jnp.float32).astype(jnp.bfloat16)
        return total + weight[:, None] * result.astype(jnp.float32), None

    start = jnp.zeros(tokens.shape, jnp.float32)
    total, unused = lax.scan(one_expert, start, jnp.arange(EXPERTS, dtype=jnp.int32))
    return total.astype(jnp.bfloat16)
```

```python
import functools

import jax
import jax.numpy as jnp
import numpy as np
from jax import lax
from jax.experimental import pallas as pl
from jax.experimental.pallas import tpu as pltpu
from jax.sharding import PartitionSpec as P

TENSOR = 16
MASKS = (1, 3, 4, 12)
CHAINS = ((0, 2, 1, 3), (1, 3, 0, 2), (2, 0, 3, 1), (3, 1, 2, 0))
MIB = 1 << 20


def positions(masks):
    table = [0] * TENSOR
    for bits in range(TENSOR):
        r = 0
        for k in range(4):
            if bits >> k & 1:
                r ^= masks[k]
        table[r] = bits
    return table


GATHER_POS = [positions([MASKS[l] for l in order]) for order in CHAINS]
SCATTER_POS = [positions([MASKS[l] for l in order]) for order in CHAINS]


def linear(table, value):
    total = 0
    for bit in range(4):
        total = total ^ (((value >> bit) & 1) * table[1 << bit])
    return total


def exchange(value, link):
    pairs = [(t, t ^ MASKS[link]) for t in range(TENSOR)]
    return lax.ppermute(value, "tensor", pairs)


def dispatch_kernel(core_ref, ids_ref, tok_ref, own_ref, oth_ref, pos_ref):
    rows = tok_ref.shape[0]
    cap = own_ref.shape[0]
    core = core_ref[0]
    first, second = ids_ref[:, 0:1], ids_ref[:, 1:2]
    tri = (
        lax.broadcasted_iota(jnp.int32, (rows, rows), 0) > lax.broadcasted_iota(jnp.int32, (rows, rows), 1)
    ).astype(jnp.bfloat16)
    lane = lax.broadcasted_iota(jnp.int32, (rows, 128), 1)
    wanted = jnp.where(lane == 0, core, jnp.where(lane == 1, 1 - core, -1))
    match = ((first == wanted) | (second == wanted)).astype(jnp.bfloat16)
    earlier = jnp.dot(tri, match, preferred_element_type=jnp.float32).astype(jnp.int32)
    slot = jnp.where(match > 0, earlier, -1)
    pos_ref[...] = slot
    slots = lax.broadcasted_iota(jnp.int32, (rows, cap), 1)
    for k, out in enumerate((own_ref, oth_ref)):
        onehot = (slot[:, k : k + 1] == slots).astype(jnp.bfloat16)
        picked = lax.dot_general(
            onehot, tok_ref[...], (((0,), (0,)), ((), ())), preferred_element_type=jnp.float32
        )
        out[...] = picked.astype(jnp.bfloat16)


def dispatch(core, ids, tokens, cap):
    rows, width = tokens.shape
    vmem = pl.BlockSpec(memory_space=pltpu.VMEM)
    return pl.pallas_call(
        dispatch_kernel,
        in_specs=[pl.BlockSpec(memory_space=pltpu.SMEM), vmem, vmem],
        out_specs=[vmem, vmem, vmem],
        out_shape=[
            jax.ShapeDtypeStruct((cap, width), jnp.bfloat16),
            jax.ShapeDtypeStruct((cap, width), jnp.bfloat16),
            jax.ShapeDtypeStruct((rows, 128), jnp.int32),
        ],
        name="dispatch",
    )(core, ids, tokens)


def combine_kernel(core_ref, ids_ref, gates_ref, pos_ref, own_ref, oth_ref, out_ref):
    rows = ids_ref.shape[0]
    cap = own_ref.shape[0]
    core = core_ref[0]
    slots = lax.broadcasted_iota(jnp.int32, (rows, cap), 1)
    total = jnp.zeros(out_ref.shape, jnp.float32)
    for k, src in enumerate((own_ref, oth_ref)):
        expert = core if k == 0 else 1 - core
        weight = jnp.sum(jnp.where(ids_ref[...] == expert, gates_ref[...], 0.0), axis=1, keepdims=True)
        onehot = (pos_ref[:, k : k + 1] == slots).astype(jnp.bfloat16)
        total += weight * jnp.dot(onehot, src[...], preferred_element_type=jnp.float32)
    out_ref[...] = total.astype(jnp.bfloat16)


def combine(core, ids, gates, slot, own, oth):
    vmem = pl.BlockSpec(memory_space=pltpu.VMEM)
    return pl.pallas_call(
        combine_kernel,
        in_specs=[pl.BlockSpec(memory_space=pltpu.SMEM)] + [vmem] * 5,
        out_specs=vmem,
        out_shape=jax.ShapeDtypeStruct((ids.shape[0], own.shape[1]), jnp.bfloat16),
        name="combine",
    )(core, ids, gates, slot, own, oth)


def expert_kernel(me_ref, x0, x1, x2, x3, wg_ref, wu_ref, wd_ref, *rest):
    sends, keeps = rest[0:4], rest[4:8]
    acc_g, acc_u, gated, xs = rest[8:]
    step = pl.program_id(0)
    me = me_ref[0]
    part, width = x0.shape[1], x0.shape[2]

    @pl.when(step < 8)
    def _():
        for half in range(2):
            block = 2 * step + half
            for i, x in enumerate((x0, x1, x2, x3)):
                where = linear(GATHER_POS[i], block ^ me)
                xs[i * part : (i + 1) * part, half * width : (half + 1) * width] = x[where]
        g = jnp.dot(xs[...], wg_ref[...], preferred_element_type=jnp.float32)
        u = jnp.dot(xs[...], wu_ref[...], preferred_element_type=jnp.float32)

        @pl.when(step == 0)
        def _():
            acc_g[...] = g
            acc_u[...] = u

        @pl.when(step > 0)
        def _():
            acc_g[...] += g
            acc_u[...] += u

    @pl.when(step == 7)
    def _():
        v = acc_g[...]
        gated[...] = (v / (1.0 + jnp.exp(-v)) * acc_u[...]).astype(jnp.bfloat16)

    @pl.when(step >= 8)
    def _():
        y = jnp.dot(gated[...], wd_ref[...], preferred_element_type=jnp.float32)
        for half in range(2):
            block = 2 * (step - 8) + half
            for i in range(4):
                where = linear(SCATTER_POS[i], block ^ me)
                piece = y[i * part : (i + 1) * part, half * width : (half + 1) * width]

                @pl.when(where >= 8)
                def _():
                    sends[i][where - 8] = piece.astype(jnp.bfloat16)

                @pl.when(where < 8)
                def _():
                    keeps[i][where] = piece


def experts(me, xs, w_gate, w_up, w_down):
    blocks, part, width = xs[0].shape
    rows = 4 * part
    model, hidden = w_gate.shape
    pair = 2 * width
    vmem = pl.BlockSpec(memory_space=pltpu.VMEM)
    return pl.pallas_call(
        expert_kernel,
        grid=(16,),
        in_specs=[pl.BlockSpec(memory_space=pltpu.SMEM)]
        + [vmem] * 4
        + [
            pl.BlockSpec((pair, hidden), lambda s: (jnp.minimum(s, 7), 0)),
            pl.BlockSpec((pair, hidden), lambda s: (jnp.minimum(s, 7), 0)),
            pl.BlockSpec((hidden, pair), lambda s: (0, jnp.maximum(s - 8, 0))),
        ],
        out_specs=[vmem] * 8,
        out_shape=[jax.ShapeDtypeStruct((8, part, width), jnp.bfloat16)] * 4
        + [jax.ShapeDtypeStruct((8, part, width), jnp.float32)] * 4,
        scratch_shapes=[
            pltpu.VMEM((rows, hidden), jnp.float32),
            pltpu.VMEM((rows, hidden), jnp.float32),
            pltpu.VMEM((rows, hidden), jnp.bfloat16),
            pltpu.VMEM((rows, pair), jnp.bfloat16),
        ],
        compiler_params=pltpu.CompilerParams(vmem_limit_bytes=48 * MIB),
        cost_estimate=pl.CostEstimate(
            flops=6 * rows * model * hidden, bytes_accessed=6 * model * hidden, transcendentals=rows * hidden
        ),
        name="experts",
    )(me, *xs, w_gate, w_up, w_down)


def body(tokens, route_ids, route_gates, w_gate, w_up, w_down):
    rows, width = tokens.shape
    cap = rows // 2
    part = cap // 2
    swap = [(0, 1), (1, 0)]
    core = lax.axis_index("expert").astype(jnp.int32).reshape(1)
    me = lax.axis_index("tensor").astype(jnp.int32).reshape(1)

    own, oth, slot = dispatch(core, route_ids, tokens, cap)
    got = lax.ppermute(oth, "expert", swap)
    held = [own[None, :part], own[None, part:], got[None, :part], got[None, part:]]
    for phase in range(4):
        arrived = [exchange(held[i], CHAINS[i][phase]) for i in range(4)]
        held = [jnp.concatenate([held[i], arrived[i]]) for i in range(4)]

    results = experts(me, held, w_gate[0], w_up[0], w_down[0])
    sends, keeps = list(results[:4]), list(results[4:])
    for phase in range(4):
        link = [CHAINS[i][3 - phase] for i in range(4)]
        arrived = [exchange(sends[i], link[i]) for i in range(4)]
        sums = [keeps[i] + arrived[i].astype(jnp.float32) for i in range(4)]
        half = sums[0].shape[0] // 2
        if phase < 3:
            sends = [s[half:].astype(jnp.bfloat16) for s in sums]
            keeps = [s[:half] for s in sums]
    done = [s[0].astype(jnp.bfloat16) for s in sums]
    mine = jnp.concatenate(done[:2])
    theirs = jnp.concatenate(done[2:])
    back = lax.ppermute(theirs, "expert", swap)
    return combine(core, route_ids, route_gates, slot, mine, back)


def solution(mesh):
    placed = (
        P(("dp", "expert"), "tensor"),
        P(("dp", "expert"), None),
        P(("dp", "expert"), None),
        P("expert", None, "tensor"),
        P("expert", None, "tensor"),
        P("expert", "tensor", None),
    )
    return jax.shard_map(
        body, mesh=mesh, in_specs=placed, out_specs=P(("dp", "expert"), "tensor"), check_vma=False
    )
```

```python
import jax
import jax.numpy as jnp
from jax import lax
from jax.experimental import pallas as pl
from jax.experimental.pallas import tpu as pltpu
from jax.sharding import PartitionSpec as P

TENSOR = 16
MASKS = (1, 3, 4, 12)
VMEM_LIMIT = 16 << 20


CHAINS = (((0, 2, 1, 3), (1, 3, 0, 2)), ((2, 0, 3, 1), (3, 1, 2, 0)))
SWAP = [(0, 1), (1, 0)]


def mask_of(core, chain, bits):
    mask = 0
    for phase in range(4):
        if bits >> phase & 1:
            mask ^= MASKS[CHAINS[core][chain][phase]]
    return mask


def block_of(core, me, chain, bits):
    return me ^ jnp.where(core == 0, mask_of(0, chain, bits), mask_of(1, chain, bits))


def exchange(value, chain, bits):
    pairs = []
    for core in range(2):
        mask = mask_of(core, chain, bits)
        pairs += [(core * TENSOR + t, core * TENSOR + (t ^ mask)) for t in range(TENSOR)]
    return lax.ppermute(value, ("expert", "tensor"), pairs)


together = lax.optimization_barrier


def exchange_pair(values, bits):
    values = together(list(values))
    return together([exchange(values[i], i, bits) for i in range(2)])


def dispatch_kernel(core_ref, ids_ref, tok_ref, own_ref, oth_ref, pos_ref):
    rows = tok_ref.shape[0]
    cap = own_ref.shape[0]
    core = core_ref[0]
    first, second = ids_ref[:, 0:1], ids_ref[:, 1:2]
    tri = (
        lax.broadcasted_iota(jnp.int32, (rows, rows), 0) > lax.broadcasted_iota(jnp.int32, (rows, rows), 1)
    ).astype(jnp.bfloat16)
    lane = lax.broadcasted_iota(jnp.int32, (rows, 128), 1)
    wanted = jnp.where(lane == 0, core, jnp.where(lane == 1, 1 - core, -1))
    match = ((first == wanted) | (second == wanted)).astype(jnp.bfloat16)
    earlier = jnp.dot(tri, match, preferred_element_type=jnp.float32).astype(jnp.int32)
    slot = jnp.where(match > 0, earlier, -1)
    pos_ref[...] = slot
    slots = lax.broadcasted_iota(jnp.int32, (rows, cap), 1)
    for k, out in enumerate((own_ref, oth_ref)):
        onehot = (slot[:, k : k + 1] == slots).astype(jnp.bfloat16)
        picked = lax.dot_general(
            onehot, tok_ref[...], (((0,), (0,)), ((), ())), preferred_element_type=jnp.float32
        )
        out[...] = picked.astype(jnp.bfloat16)


def dispatch(core, ids, tokens, cap):
    rows, width = tokens.shape
    vmem = pl.BlockSpec(memory_space=pltpu.VMEM)
    return pl.pallas_call(
        dispatch_kernel,
        in_specs=[pl.BlockSpec(memory_space=pltpu.SMEM), vmem, vmem],
        out_specs=[vmem, vmem, vmem],
        out_shape=[
            jax.ShapeDtypeStruct((cap, width), jnp.bfloat16),
            jax.ShapeDtypeStruct((cap, width), jnp.bfloat16),
            jax.ShapeDtypeStruct((rows, 128), jnp.int32),
        ],
        name="dispatch",
    )(core, ids, tokens)


def combine_kernel(core_ref, ids_ref, gates_ref, pos_ref, own_ref, oth_ref, out_ref):
    rows = ids_ref.shape[0]
    cap = own_ref.shape[0]
    core = core_ref[0]
    slots = lax.broadcasted_iota(jnp.int32, (rows, cap), 1)
    total = jnp.zeros(out_ref.shape, jnp.float32)
    for k, src in enumerate((own_ref, oth_ref)):
        expert = core if k == 0 else 1 - core
        weight = jnp.sum(jnp.where(ids_ref[...] == expert, gates_ref[...], 0.0), axis=1, keepdims=True)
        onehot = (pos_ref[:, k : k + 1] == slots).astype(jnp.bfloat16)
        total += weight * jnp.dot(onehot, src[...], preferred_element_type=jnp.float32)
    out_ref[...] = total.astype(jnp.bfloat16)


def combine(core, ids, gates, slot, own, oth):
    vmem = pl.BlockSpec(memory_space=pltpu.VMEM)
    return pl.pallas_call(
        combine_kernel,
        in_specs=[pl.BlockSpec(memory_space=pltpu.SMEM)] + [vmem] * 5,
        out_specs=vmem,
        out_shape=jax.ShapeDtypeStruct((ids.shape[0], own.shape[1]), jnp.bfloat16),
        name="combine",
    )(core, ids, gates, slot, own, oth)


def add_blocks(here_ref, pieces, wg, wu, acc_g, acc_u, fresh):
    core, me = here_ref[0], here_ref[1]
    rows, width = pieces[0][2].shape[1:]
    hidden = wg.shape[1]
    tile = hidden // 2
    for chain in range(2):
        at = slice(chain * rows, (chain + 1) * rows)
        for acc, w in ((acc_g, wg), (acc_u, wu)):
            for n in range(2):
                cols = slice(n * tile, (n + 1) * tile)
                total = jnp.zeros((rows, tile), jnp.float32) if fresh else acc[at, cols]
                for owner, first, ref in pieces:
                    if owner != chain:
                        continue
                    for k in range(ref.shape[0]):
                        start = pl.multiple_of(block_of(core, me, chain, first + k) * width, width)
                        total += jnp.dot(
                            ref[k], w[pl.ds(start, width), cols], preferred_element_type=jnp.float32
                        )
                yield acc, at, cols, total


def early_kernel(here_ref, ha, hb, ta, tb, fa, fb, wg, wu, acc_g, acc_u):
    pieces = [(0, 0, ha), (1, 0, hb), (0, 4, ta), (1, 4, tb), (0, 8, fa), (1, 8, fb)]
    for acc, at, cols, total in add_blocks(here_ref, pieces, wg, wu, acc_g, acc_u, True):
        acc[at, cols] = total


def down_blocks(here_ref, gated, wd, first, outs):
    core, me = here_ref[0], here_ref[1]
    count, rows, width = outs[0].shape
    for chain in range(2):
        for k in range(count):
            start = pl.multiple_of(block_of(core, me, chain, first + k) * width, width)
            y = jnp.dot(
                gated[chain * rows : (chain + 1) * rows, :],
                wd[:, pl.ds(start, width)],
                preferred_element_type=jnp.float32,
            )
            outs[chain][k] = y.astype(outs[chain].dtype)


def middle_kernel(here_ref, la, lb, acc_g, acc_u, wg, wu, wd, gated, sa, sb):
    pieces = [(0, 12, la), (1, 12, lb)]
    sums = {}
    for acc, at, cols, total in add_blocks(here_ref, pieces, wg, wu, acc_g, acc_u, False):
        if acc is acc_g:
            sums[at.start, cols.start] = total
        else:
            v = sums.pop((at.start, cols.start))
            gated[at, cols] = (v / (1.0 + jnp.exp(-v)) * total).astype(jnp.bfloat16)
    down_blocks(here_ref, gated, wd, 12, (sa, sb))


def late_kernel(here_ref, gated, wd, sa, sb, ka, kb, ra, rb):
    down_blocks(here_ref, gated, wd, 8, (sa, sb))
    down_blocks(here_ref, gated, wd, 4, (ka, kb))
    down_blocks(here_ref, gated, wd, 0, (ra, rb))


def local_kernel(kernel, name, cost, outs, here, *operands):
    vmem = pl.BlockSpec(memory_space=pltpu.VMEM)
    return pl.pallas_call(
        kernel,
        in_specs=[pl.BlockSpec(memory_space=pltpu.SMEM)] + [vmem] * len(operands),
        out_specs=[vmem] * len(outs),
        out_shape=[jax.ShapeDtypeStruct(shape, dtype) for shape, dtype in outs],
        compiler_params=pltpu.CompilerParams(vmem_limit_bytes=VMEM_LIMIT),
        cost_estimate=pl.CostEstimate(flops=cost, bytes_accessed=1 << 16, transcendentals=0),
        name=name,
    )(here, *operands)


def body(tokens, route_ids, route_gates, w_gate, w_up, w_down):
    rows, width = tokens.shape
    cap = rows // 2
    part = cap // 2
    hidden = w_gate.shape[2]
    wg, wu, wd = w_gate[0], w_up[0], w_down[0]
    core = lax.axis_index("expert").astype(jnp.int32).reshape(1)
    here = jnp.stack([lax.axis_index("expert"), lax.axis_index("tensor")]).astype(jnp.int32)
    both = range(2)

    own, oth, slot = dispatch(core, route_ids, tokens, cap)
    got = lax.ppermute(oth, "expert", SWAP)
    mine = [jnp.concatenate([v[i * part : (i + 1) * part] for v in (own, got)]) for i in both]
    mine = together(mine)
    near = together([[exchange(mine[i], i, bits) for bits in (1, 2, 3)] for i in both])
    held = together([jnp.stack([mine[i], *near[i]]) for i in both])
    third = exchange_pair(held, 4)
    fourth = exchange_pair(held, 8)
    last = exchange_pair(third, 8)

    bf16, f32 = jnp.bfloat16, jnp.float32
    block, square = (4, cap, width), (rows, hidden)
    sums = local_kernel(early_kernel, "early", 1 << 33, [(square, f32)] * 2, here, *held, *third, *fourth, wg, wu)
    gated, *send = local_kernel(
        middle_kernel, "middle", 1 << 32, [(square, bf16)] + [(block, bf16)] * 2, here, *last, *sums, wg, wu, wd
    )
    gone = exchange_pair(send, 8)
    out = local_kernel(late_kernel, "late", 1 << 20, [(block, bf16)] * 2 + [(block, f32)] * 4, here, gated, wd)
    also = exchange_pair(out[0:2], 8)
    second = exchange_pair([(out[2 + i] + gone[i].astype(f32)).astype(bf16) for i in both], 4)
    total = [out[4 + i] + also[i].astype(f32) + second[i].astype(f32) for i in both]
    send = together([total[i].astype(bf16) for i in both])
    near = together([[exchange(send[i][bits], i, bits) for bits in (1, 2, 3)] for i in both])
    done = [
        (total[i][0] + near[i][0].astype(f32) + near[i][1].astype(f32) + near[i][2].astype(f32)).astype(bf16)
        for i in both
    ]
    kept = jnp.concatenate([d[:part] for d in done])
    theirs = jnp.concatenate([d[part:] for d in done])
    back = lax.ppermute(theirs, "expert", SWAP)
    return combine(core, route_ids, route_gates, slot, kept, back)


def solution(mesh):
    placed = (
        P(("dp", "expert"), "tensor"),
        P(("dp", "expert"), None),
        P(("dp", "expert"), None),
        P("expert", None, "tensor"),
        P("expert", None, "tensor"),
        P("expert", "tensor", None),
    )
    return jax.shard_map(
        body, mesh=mesh, in_specs=placed, out_specs=P(("dp", "expert"), "tensor"), check_vma=False
    )
```

```python
import jax
import jax.numpy as jnp
from jax import lax
from jax.experimental import pallas as pl
from jax.experimental.pallas import tpu as pltpu
from jax.sharding import PartitionSpec as P

TENSOR = 16
MASKS = (1, 3, 4, 12)
VMEM_LIMIT = 16 << 20
LOAD_VMEM = 32 << 20
LOAD, EARLY, MIDDLE, LATE = 1 << 33, 1 << 33, 1 << 32, 1 << 20


CHAINS = (((0, 2, 1, 3), (1, 3, 0, 2)), ((1, 3, 2, 0), (0, 2, 3, 1)))
SWAP = [(0, 1), (1, 0)]


def mask_of(core, chain, bits):
    mask = 0
    for phase in range(4):
        if bits >> phase & 1:
            mask ^= MASKS[CHAINS[core][chain][phase]]
    return mask


def block_of(core, me, chain, bits):
    return me ^ jnp.where(core == 0, mask_of(0, chain, bits), mask_of(1, chain, bits))


def exchange(value, chain, bits):
    pairs = []
    for core in range(2):
        mask = mask_of(core, chain, bits)
        pairs += [(core * TENSOR + t, core * TENSOR + (t ^ mask)) for t in range(TENSOR)]
    return lax.ppermute(value, ("expert", "tensor"), pairs)


together = lax.optimization_barrier


def exchange_pair(values, bits):
    values = together(list(values))
    return together([exchange(values[i], i, bits) for i in range(2)])


def dispatch_kernel(core_ref, ids_ref, tok_ref, out_ref, slot_ref):
    rows = tok_ref.shape[0]
    cap = out_ref.shape[0] // 2
    core = core_ref[0]
    kinds = slot_ref.shape[0]
    tri = (
        lax.broadcasted_iota(jnp.int32, (rows, rows), 0) < lax.broadcasted_iota(jnp.int32, (rows, rows), 1)
    ).astype(jnp.bfloat16)
    kind = lax.broadcasted_iota(jnp.int32, (kinds, rows), 0)
    wanted = jnp.where(kind == 0, core, jnp.where(kind == 1, 1 - core, -1))
    match = ((ids_ref[0:1, :] == wanted) | (ids_ref[1:2, :] == wanted)).astype(jnp.bfloat16)
    earlier = jnp.dot(match, tri, preferred_element_type=jnp.float32).astype(jnp.int32)
    slot = jnp.where(match > 0, earlier, -1)
    slot_ref[...] = slot
    slots = lax.broadcasted_iota(jnp.int32, (cap, rows), 0)
    for k in range(2):
        onehot = (slot[k : k + 1, :] == slots).astype(jnp.bfloat16)
        picked = jnp.dot(onehot, tok_ref[...], preferred_element_type=jnp.float32)
        out_ref[k * cap : (k + 1) * cap, :] = picked.astype(jnp.bfloat16)


def dispatch(core, ids, tokens):
    rows, width = tokens.shape
    vmem = pl.BlockSpec(memory_space=pltpu.VMEM)
    return pl.pallas_call(
        dispatch_kernel,
        in_specs=[pl.BlockSpec(memory_space=pltpu.SMEM), vmem, vmem],
        out_specs=[vmem, vmem],
        out_shape=[
            jax.ShapeDtypeStruct((rows, width), jnp.bfloat16),
            jax.ShapeDtypeStruct((16, rows), jnp.int32),
        ],
        name="dispatch",
    )(core, ids, tokens)


def weigh_kernel(core_ref, ids_ref, gates_ref, slot_ref, pick_ref, weight_ref):
    rows = pick_ref.shape[0]
    cap = pick_ref.shape[1] // 2
    core = core_ref[0]
    kind = lax.broadcasted_iota(jnp.int32, (128, rows), 0)
    wanted = jnp.where(kind == 0, core, jnp.where(kind == 1, 1 - core, -1))
    weight = jnp.where(ids_ref[0:1, :] == wanted, gates_ref[0:1, :], 0.0)
    weight += jnp.where(ids_ref[1:2, :] == wanted, gates_ref[1:2, :], 0.0)
    weight_ref[...] = weight.T
    slot = jnp.where(kind == 0, slot_ref[0:1, :], slot_ref[1:2, :]).astype(jnp.float32).T
    slots = lax.broadcasted_iota(jnp.int32, (rows, cap), 1).astype(jnp.float32)
    for k in range(2):
        pick_ref[:, k * cap : (k + 1) * cap] = (slot[:, k : k + 1] == slots).astype(jnp.bfloat16)


def weigh(core, ids, gates, slot):
    rows = ids.shape[1]
    vmem = pl.BlockSpec(memory_space=pltpu.VMEM)
    return pl.pallas_call(
        weigh_kernel,
        in_specs=[pl.BlockSpec(memory_space=pltpu.SMEM)] + [vmem] * 3,
        out_specs=[vmem, vmem],
        out_shape=[
            jax.ShapeDtypeStruct((rows, rows), jnp.bfloat16),
            jax.ShapeDtypeStruct((rows, 128), jnp.float32),
        ],
        cost_estimate=pl.CostEstimate(flops=1 << 30, bytes_accessed=1 << 16, transcendentals=0),
        name="weigh",
    )(core, ids, gates, slot)


def combine_kernel(pick_ref, weight_ref, own_ref, back_ref, na_ref, nb_ref, nc_ref, out_ref):
    cap = own_ref.shape[1]
    total = jnp.zeros(out_ref.shape, jnp.float32)
    for k, first in enumerate((own_ref, back_ref)):
        at = slice(k * cap, (k + 1) * cap)
        done = first[0].astype(jnp.float32)
        for ref in (na_ref, nb_ref, nc_ref):
            done += ref[at, :].astype(jnp.float32)
        row = jnp.dot(pick_ref[:, at], done.astype(jnp.bfloat16), preferred_element_type=jnp.float32)
        total += weight_ref[:, k : k + 1] * row
    out_ref[...] = total.astype(jnp.bfloat16)


def combine(pick, weight, own, back, near):
    vmem = pl.BlockSpec(memory_space=pltpu.VMEM)
    return pl.pallas_call(
        combine_kernel,
        in_specs=[vmem] * 7,
        out_specs=vmem,
        out_shape=jax.ShapeDtypeStruct((pick.shape[0], own.shape[2]), jnp.bfloat16),
        name="combine",
    )(pick, weight, own, back, *near)


def load_kernel(here_ref, *refs):
    sources, targets, sem = refs[:3], refs[3:6], refs[6]
    copies = [pltpu.make_async_copy(a, b, sem.at[i]) for i, (a, b) in enumerate(zip(sources, targets))]
    for copy in copies:
        copy.start()
    for copy in copies:
        copy.wait()


def load(here, *weights):
    vmem = pl.BlockSpec(memory_space=pltpu.VMEM)
    hbm = pl.BlockSpec(memory_space=pl.ANY)
    return pl.pallas_call(
        load_kernel,
        in_specs=[pl.BlockSpec(memory_space=pltpu.SMEM)] + [hbm] * 3,
        out_specs=[vmem] * 3,
        out_shape=[jax.ShapeDtypeStruct(w.shape, w.dtype) for w in weights],
        scratch_shapes=[pltpu.SemaphoreType.DMA((3,))],
        compiler_params=pltpu.CompilerParams(vmem_limit_bytes=LOAD_VMEM),
        cost_estimate=pl.CostEstimate(flops=LOAD, bytes_accessed=1 << 16, transcendentals=0),
        name="load",
    )(here, *weights)


def add_blocks(here_ref, pieces, wg, wu, acc_g, acc_u, fresh):
    core, me = here_ref[0], here_ref[1]
    rows, width = pieces[0][2].shape[1:]
    hidden = wg.shape[1]
    tile = hidden // 2
    for chain in range(2):
        at = slice(chain * rows, (chain + 1) * rows)
        for acc, w in ((acc_g, wg), (acc_u, wu)):
            for n in range(2):
                cols = slice(n * tile, (n + 1) * tile)
                total = jnp.zeros((rows, tile), jnp.float32) if fresh else acc[at, cols]
                for owner, first, ref in pieces:
                    if owner != chain:
                        continue
                    for k in range(ref.shape[0]):
                        start = pl.multiple_of(block_of(core, me, chain, first + k) * width, width)
                        total += jnp.dot(
                            ref[k], w[pl.ds(start, width), cols], preferred_element_type=jnp.float32
                        )
                yield acc, at, cols, total


def early_kernel(here_ref, ha, hb, ta, tb, fa, fb, wg, wu, acc_g, acc_u):
    pieces = [(0, 0, ha), (1, 0, hb), (0, 4, ta), (1, 4, tb), (0, 8, fa), (1, 8, fb)]
    for acc, at, cols, total in add_blocks(here_ref, pieces, wg, wu, acc_g, acc_u, True):
        acc[at, cols] = total


def down_blocks(here_ref, gated, wd, first, outs):
    core, me = here_ref[0], here_ref[1]
    count, rows, width = outs[0].shape
    for chain in range(2):
        for k in range(count):
            start = pl.multiple_of(block_of(core, me, chain, first + k) * width, width)
            y = jnp.dot(
                gated[chain * rows : (chain + 1) * rows, :],
                wd[:, pl.ds(start, width)],
                preferred_element_type=jnp.float32,
            )
            outs[chain][k] = y.astype(outs[chain].dtype)


def middle_kernel(here_ref, la, lb, acc_g, acc_u, wg, wu, wd, gated, sa, sb):
    pieces = [(0, 12, la), (1, 12, lb)]
    sums = {}
    for acc, at, cols, total in add_blocks(here_ref, pieces, wg, wu, acc_g, acc_u, False):
        if acc is acc_g:
            sums[at.start, cols.start] = total
        else:
            v = sums.pop((at.start, cols.start))
            gated[at, cols] = (v / (1.0 + jnp.exp(-v)) * total).astype(jnp.bfloat16)
    down_blocks(here_ref, gated, wd, 12, (sa, sb))


def late_kernel(here_ref, gated, wd, sa, sb, ka, kb, ra, rb):
    down_blocks(here_ref, gated, wd, 8, (sa, sb))
    down_blocks(here_ref, gated, wd, 4, (ka, kb))
    down_blocks(here_ref, gated, wd, 0, (ra, rb))


def local_kernel(kernel, name, cost, outs, here, *operands):
    vmem = pl.BlockSpec(memory_space=pltpu.VMEM)
    return pl.pallas_call(
        kernel,
        in_specs=[pl.BlockSpec(memory_space=pltpu.SMEM)] + [vmem] * len(operands),
        out_specs=[vmem] * len(outs),
        out_shape=[jax.ShapeDtypeStruct(shape, dtype) for shape, dtype in outs],
        compiler_params=pltpu.CompilerParams(vmem_limit_bytes=VMEM_LIMIT),
        cost_estimate=pl.CostEstimate(flops=cost, bytes_accessed=1 << 16, transcendentals=0),
        name=name,
    )(here, *operands)


def body(tokens, route_ids, route_gates, w_gate, w_up, w_down):
    rows, width = tokens.shape
    cap = rows // 2
    part = cap // 2
    hidden = w_gate.shape[2]
    wg, wu, wd = w_gate[0], w_up[0], w_down[0]
    core = lax.axis_index("expert").astype(jnp.int32).reshape(1)
    here = jnp.stack([lax.axis_index("expert"), lax.axis_index("tensor")]).astype(jnp.int32)
    both = range(2)

    bf16, f32 = jnp.bfloat16, jnp.float32
    block, square = (4, cap, width), (rows, hidden)

    bf16, f32 = jnp.bfloat16, jnp.float32
    block, square = (4, cap, width), (rows, hidden)

    ids, gates = route_ids.T, route_gates.T
    mine, slot = dispatch(core, ids, tokens)
    near = together([exchange(mine, 0, bits) for bits in (1, 2, 3)])
    own, oth = together([jnp.stack([x[i * cap : (i + 1) * cap] for x in (mine, *near)]) for i in both])
    held = [own, lax.ppermute(oth, "expert", SWAP)]
    held, there, slot = together((held, here, slot))
    wg, wu, wd = load(there, wg, wu, wd)
    pick, weight = weigh(core, ids, gates, slot)
    third = exchange_pair(held, 4)
    fourth = exchange_pair(held, 8)
    last = exchange_pair(third, 8)
    third, pick, weight = together((third, pick, weight))
    sums = local_kernel(
        early_kernel, "early", EARLY, [(square, f32)] * 2, here, *held, *third, *fourth, wg, wu
    )
    gated, *send = local_kernel(
        middle_kernel, "middle", MIDDLE, [(square, bf16)] + [(block, bf16)] * 2, here, *last, *sums, wg, wu, wd
    )
    gone = exchange_pair(send, 8)
    out = local_kernel(late_kernel, "late", LATE, [(block, bf16)] * 2 + [(block, f32)] * 4, here, gated, wd)
    also = exchange_pair(out[0:2], 8)
    second = exchange_pair([(out[2 + i] + gone[i].astype(f32)).astype(bf16) for i in both], 4)
    total = [out[4 + i] + also[i].astype(f32) + second[i].astype(f32) for i in both]
    own, oth = together(total)
    back = lax.ppermute(oth.astype(bf16), "expert", SWAP)
    own, back = together((own, back))
    send = [jnp.concatenate([own[bits].astype(bf16), back[bits]]) for bits in (1, 2, 3)]
    send = together(send)
    near = together([exchange(x, 0, bits) for bits, x in zip((1, 2, 3), send)])
    return combine(pick, weight, own[:1], back[:1], near)


def solution(mesh):
    placed = (
        P(("dp", "expert"), "tensor"),
        P(("dp", "expert"), None),
        P(("dp", "expert"), None),
        P("expert", None, "tensor"),
        P("expert", None, "tensor"),
        P("expert", "tensor", None),
    )
    return jax.shard_map(
        body, mesh=mesh, in_specs=placed, out_specs=P(("dp", "expert"), "tensor"), check_vma=False
    )
```

```python
import functools

import jax
import jax.numpy as jnp
from jax import lax
from jax.experimental import pallas as pl
from jax.experimental.pallas import tpu as pltpu
from jax.sharding import PartitionSpec as P

TENSOR = 16
MASKS = (1, 3, 4, 12)
VMEM_LIMIT = 8 << 20
LOAD_VMEM = 32 << 20
LOAD, EARLY, MIDDLE, LATE = 1 << 33, (1 << 32, 1 << 20), 1 << 20, 1 << 31


CHAINS = (((0, 2, 1, 3), (1, 3, 0, 2)), ((1, 3, 2, 0), (0, 2, 3, 1)))
SWAP = [(0, 1), (1, 0)]


def mask_of(core, chain, bits):
    mask = 0
    for phase in range(4):
        if bits >> phase & 1:
            mask ^= MASKS[CHAINS[core][chain][phase]]
    return mask


def block_of(core, me, chain, bits):
    return me ^ jnp.where(core == 0, mask_of(0, chain, bits), mask_of(1, chain, bits))


def exchange(value, chain, bits):
    pairs = []
    for core in range(2):
        mask = mask_of(core, chain, bits)
        pairs += [(core * TENSOR + t, core * TENSOR + (t ^ mask)) for t in range(TENSOR)]
    return lax.ppermute(value, ("expert", "tensor"), pairs)


together = lax.optimization_barrier


def dispatch_kernel(core_ref, ids_ref, tok_ref, out_ref, slot_ref):
    rows = tok_ref.shape[0]
    cap = out_ref.shape[0] // 2
    core = core_ref[0]
    kinds = slot_ref.shape[0]
    tri = (
        lax.broadcasted_iota(jnp.int32, (rows, rows), 0) < lax.broadcasted_iota(jnp.int32, (rows, rows), 1)
    ).astype(jnp.bfloat16)
    kind = lax.broadcasted_iota(jnp.int32, (kinds, rows), 0)
    wanted = jnp.where(kind == 0, core, jnp.where(kind == 1, 1 - core, -1))
    match = ((ids_ref[0:1, :] == wanted) | (ids_ref[1:2, :] == wanted)).astype(jnp.bfloat16)
    earlier = jnp.dot(match, tri, preferred_element_type=jnp.float32).astype(jnp.int32)
    slot = jnp.where(match > 0, earlier, -1)
    slot_ref[...] = slot
    slots = lax.broadcasted_iota(jnp.int32, (cap, rows), 0)
    for k in range(2):
        onehot = (slot[k : k + 1, :] == slots).astype(jnp.bfloat16)
        picked = jnp.dot(onehot, tok_ref[...], preferred_element_type=jnp.float32)
        out_ref[k * cap : (k + 1) * cap, :] = picked.astype(jnp.bfloat16)


def dispatch(core, ids, tokens):
    rows, width = tokens.shape
    vmem = pl.BlockSpec(memory_space=pltpu.VMEM)
    return pl.pallas_call(
        dispatch_kernel,
        in_specs=[pl.BlockSpec(memory_space=pltpu.SMEM), vmem, vmem],
        out_specs=[vmem, vmem],
        out_shape=[
            jax.ShapeDtypeStruct((rows, width), jnp.bfloat16),
            jax.ShapeDtypeStruct((16, rows), jnp.int32),
        ],
        compiler_params=pltpu.CompilerParams(vmem_limit_bytes=VMEM_LIMIT),
        name="dispatch",
    )(core, ids, tokens)


def weigh_kernel(core_ref, ids_ref, gates_ref, slot_ref, pick_ref, weight_ref):
    rows = pick_ref.shape[0]
    cap = pick_ref.shape[1] // 2
    core = core_ref[0]
    kind = lax.broadcasted_iota(jnp.int32, (128, rows), 0)
    wanted = jnp.where(kind == 0, core, jnp.where(kind == 1, 1 - core, -1))
    weight = jnp.where(ids_ref[0:1, :] == wanted, gates_ref[0:1, :], 0.0)
    weight += jnp.where(ids_ref[1:2, :] == wanted, gates_ref[1:2, :], 0.0)
    weight_ref[...] = weight.T
    slot = jnp.where(kind == 0, slot_ref[0:1, :], slot_ref[1:2, :]).astype(jnp.float32).T
    slots = lax.broadcasted_iota(jnp.int32, (rows, cap), 1).astype(jnp.float32)
    for k in range(2):
        pick_ref[:, k * cap : (k + 1) * cap] = (slot[:, k : k + 1] == slots).astype(jnp.bfloat16)


def weigh(core, ids, gates, slot):
    rows = ids.shape[1]
    vmem = pl.BlockSpec(memory_space=pltpu.VMEM)
    return pl.pallas_call(
        weigh_kernel,
        in_specs=[pl.BlockSpec(memory_space=pltpu.SMEM)] + [vmem] * 3,
        out_specs=[vmem, vmem],
        out_shape=[
            jax.ShapeDtypeStruct((rows, rows), jnp.bfloat16),
            jax.ShapeDtypeStruct((rows, 128), jnp.float32),
        ],
        cost_estimate=pl.CostEstimate(flops=1 << 30, bytes_accessed=1 << 16, transcendentals=0),
        compiler_params=pltpu.CompilerParams(vmem_limit_bytes=VMEM_LIMIT),
        name="weigh",
    )(core, ids, gates, slot)


def combine_kernel(pick_ref, weight_ref, own_ref, back_ref, na_ref, nb_ref, nc_ref, out_ref):
    cap = own_ref.shape[1]
    total = jnp.zeros(out_ref.shape, jnp.float32)
    for k, first in enumerate((own_ref, back_ref)):
        at = slice(k * cap, (k + 1) * cap)
        done = first[0].astype(jnp.float32)
        for ref in (na_ref, nb_ref, nc_ref):
            done += ref[at, :].astype(jnp.float32)
        row = jnp.dot(pick_ref[:, at], done.astype(jnp.bfloat16), preferred_element_type=jnp.float32)
        total += weight_ref[:, k : k + 1] * row
    out_ref[...] = total.astype(jnp.bfloat16)


def combine(pick, weight, own, back, near):
    vmem = pl.BlockSpec(memory_space=pltpu.VMEM)
    return pl.pallas_call(
        combine_kernel,
        in_specs=[vmem] * 7,
        out_specs=vmem,
        out_shape=jax.ShapeDtypeStruct((pick.shape[0], own.shape[2]), jnp.bfloat16),
        compiler_params=pltpu.CompilerParams(vmem_limit_bytes=VMEM_LIMIT),
        name="combine",
    )(pick, weight, own, back, *near)


def load_kernel(here_ref, *refs):
    sources, targets, sem = refs[:3], refs[3:6], refs[6]
    copies = [pltpu.make_async_copy(a, b, sem.at[i]) for i, (a, b) in enumerate(zip(sources, targets))]
    for copy in copies:
        copy.start()
    for copy in copies:
        copy.wait()


def load(here, *weights):
    vmem = pl.BlockSpec(memory_space=pltpu.VMEM)
    hbm = pl.BlockSpec(memory_space=pl.ANY)
    return pl.pallas_call(
        load_kernel,
        in_specs=[pl.BlockSpec(memory_space=pltpu.SMEM)] + [hbm] * 3,
        out_specs=[vmem] * 3,
        out_shape=[jax.ShapeDtypeStruct(w.shape, w.dtype) for w in weights],
        scratch_shapes=[pltpu.SemaphoreType.DMA((3,))],
        compiler_params=pltpu.CompilerParams(vmem_limit_bytes=LOAD_VMEM),
        cost_estimate=pl.CostEstimate(flops=LOAD, bytes_accessed=1 << 16, transcendentals=0),
        name="load",
    )(here, *weights)


def add_blocks(chain, here_ref, pieces, wg, wu, acc_g=None, acc_u=None):
    core, me = here_ref[0], here_ref[1]
    rows, width = pieces[0][1].shape[1:]
    tile = wg.shape[1] // 2
    for n in range(2):
        cols = slice(n * tile, (n + 1) * tile)
        sums = []
        for acc, w in ((acc_g, wg), (acc_u, wu)):
            total = jnp.zeros((rows, tile), jnp.float32) if acc is None else acc[:, cols]
            for first, ref in pieces:
                for k in range(ref.shape[0]):
                    start = pl.multiple_of(block_of(core, me, chain, first + k) * width, width)
                    total += jnp.dot(ref[k], w[pl.ds(start, width), cols], preferred_element_type=jnp.float32)
            sums.append(total)
        yield cols, *sums


def early_kernel(chain, here_ref, held, third, fourth, wg, wu, acc_g, acc_u):
    for cols, g, u in add_blocks(chain, here_ref, [(0, held), (4, third), (8, fourth)], wg, wu):
        acc_g[:, cols] = g
        acc_u[:, cols] = u


def down_blocks(chain, here_ref, gated, wd, first, out):
    core, me = here_ref[0], here_ref[1]
    count, rows, width = out.shape
    for k in range(count):
        start = pl.multiple_of(block_of(core, me, chain, first + k) * width, width)
        y = jnp.dot(gated[...], wd[:, pl.ds(start, width)], preferred_element_type=jnp.float32)
        out[k] = y.astype(out.dtype)


def middle_kernel(chain, here_ref, last, acc_g, acc_u, wg, wu, wd, gated, send):
    for cols, g, u in add_blocks(chain, here_ref, [(12, last)], wg, wu, acc_g, acc_u):
        gated[:, cols] = (g / (1.0 + jnp.exp(-g)) * u).astype(jnp.bfloat16)
    down_blocks(chain, here_ref, gated, wd, 12, send)


def late_kernel(chain, here_ref, gated, wd, send, keep, rest):
    down_blocks(chain, here_ref, gated, wd, 8, send)
    down_blocks(chain, here_ref, gated, wd, 4, keep)
    down_blocks(chain, here_ref, gated, wd, 0, rest)


def local_kernel(kernel, name, cost, chain, outs, here, *operands):
    vmem = pl.BlockSpec(memory_space=pltpu.VMEM)
    return pl.pallas_call(
        functools.partial(kernel, chain),
        in_specs=[pl.BlockSpec(memory_space=pltpu.SMEM)] + [vmem] * len(operands),
        out_specs=[vmem] * len(outs),
        out_shape=[jax.ShapeDtypeStruct(shape, dtype) for shape, dtype in outs],
        compiler_params=pltpu.CompilerParams(vmem_limit_bytes=VMEM_LIMIT),
        cost_estimate=pl.CostEstimate(flops=cost, bytes_accessed=1 << 16, transcendentals=0),
        name=name,
    )(here, *operands)


def body(tokens, route_ids, route_gates, w_gate, w_up, w_down):
    rows, width = tokens.shape
    cap = rows // 2
    part = cap // 2
    hidden = w_gate.shape[2]
    wg, wu, wd = w_gate[0], w_up[0], w_down[0]
    core = lax.axis_index("expert").astype(jnp.int32).reshape(1)
    here = jnp.stack([lax.axis_index("expert"), lax.axis_index("tensor")]).astype(jnp.int32)
    both = range(2)

    bf16, f32 = jnp.bfloat16, jnp.float32
    block, square = (4, cap, width), (cap, hidden)

    ids, gates = route_ids.T, route_gates.T
    mine, slot = dispatch(core, ids, tokens)
    near = together([exchange(mine, 0, bits) for bits in (1, 2, 3)])
    own, oth = [jnp.stack([x[i * cap : (i + 1) * cap] for x in (mine, *near)]) for i in both]
    own, oth = together((own, oth))
    held = [own, lax.ppermute(oth, "expert", SWAP)]
    third = [exchange(held[i], i, 4) for i in both]
    held[1], own = together((held[1], own))
    fourth = [exchange(x, i, 8) for i, x in enumerate((own, held[1]))]
    own, there, slot = together((own, here, slot))
    wg, wu, wd = load(there, wg, wu, wd)
    third[0], wd = together((third[0], wd))
    last = [exchange(x, i, 8) for i, x in enumerate(third)]
    pick, weight = weigh(core, ids, gates, slot)

    third, pick, weight = together((third, pick, weight))
    early, token = [], ()
    for i in both:
        pieces, token = together(((held[i], third[i], fourth[i]), token))
        token = local_kernel(early_kernel, "early", EARLY[i], i, [(square, f32)] * 2, here, *pieces, wg, wu)
        early.append(token)
    middle, later = [], []
    for i in both:
        arrived, sums, token = together((last[i], early[i], token))
        token = local_kernel(
            middle_kernel, "middle", MIDDLE, i, [(square, bf16), (block, bf16)], here, arrived, *sums, wg, wu, wd
        )
        middle.append(token)
    for i in both:
        gated, token = together((middle[i][0], token))
        token = local_kernel(late_kernel, "late", LATE, i, [(block, bf16)] + [(block, f32)] * 2, here, gated, wd)
        later.append(token)

    total = []
    for i in both:
        send, keep, rest = later[i]
        gone = exchange(middle[i][1], i, 8)
        also = exchange(send, i, 8)
        second = exchange((keep + gone.astype(f32)).astype(bf16), i, 4)
        total.append(rest + also.astype(f32) + second.astype(f32))
    own, oth = together(total)
    back = lax.ppermute(oth.astype(bf16), "expert", SWAP)
    own, back = together((own, back))
    send = [jnp.concatenate([own[bits].astype(bf16), back[bits]]) for bits in (1, 2, 3)]
    send = together(send)
    near = together([exchange(x, 0, bits) for bits, x in zip((1, 2, 3), send)])
    return combine(pick, weight, own[:1], back[:1], near)


def solution(mesh):
    placed = (
        P(("dp", "expert"), "tensor"),
        P(("dp", "expert"), None),
        P(("dp", "expert"), None),
        P("expert", None, "tensor"),
        P("expert", None, "tensor"),
        P("expert", "tensor", None),
    )
    return jax.shard_map(
        body, mesh=mesh, in_specs=placed, out_specs=P(("dp", "expert"), "tensor"), check_vma=False
    )
```

```python
import functools

import jax
import jax.numpy as jnp
from jax import lax
from jax.experimental import pallas as pl
from jax.experimental.pallas import tpu as pltpu
from jax.sharding import PartitionSpec as P

TENSOR = 16
MASKS = (1, 3, 4, 12)
VMEM_LIMIT = 8 << 20
LOAD_VMEM = 32 << 20
LOAD, EARLY, MIDDLE, LATE = 1 << 33, (1 << 32, 1 << 20), 1 << 20, 1 << 31


CHAINS = (((0, 2, 1, 3), (1, 3, 0, 2)), ((1, 3, 2, 0), (0, 2, 3, 1)))
SWAP = [(0, 1), (1, 0)]


def mask_of(core, chain, bits):
    mask = 0
    for phase in range(4):
        if bits >> phase & 1:
            mask ^= MASKS[CHAINS[core][chain][phase]]
    return mask


def block_of(core, me, chain, bits):
    return me ^ jnp.where(core == 0, mask_of(0, chain, bits), mask_of(1, chain, bits))


def exchange(value, chain, bits):
    pairs = []
    for core in range(2):
        mask = mask_of(core, chain, bits)
        pairs += [(core * TENSOR + t, core * TENSOR + (t ^ mask)) for t in range(TENSOR)]
    return lax.ppermute(value, ("expert", "tensor"), pairs)


together = lax.optimization_barrier


def dispatch_kernel(core_ref, ids_ref, tok_ref, out_ref, slot_ref):
    rows = tok_ref.shape[0]
    cap = out_ref.shape[0] // 2
    core = core_ref[0]
    kinds = slot_ref.shape[0]
    tri = (
        lax.broadcasted_iota(jnp.int32, (rows, rows), 0) < lax.broadcasted_iota(jnp.int32, (rows, rows), 1)
    ).astype(jnp.bfloat16)
    kind = lax.broadcasted_iota(jnp.int32, (kinds, rows), 0)
    wanted = jnp.where(kind == 0, core, jnp.where(kind == 1, 1 - core, -1))
    match = ((ids_ref[0:1, :] == wanted) | (ids_ref[1:2, :] == wanted)).astype(jnp.bfloat16)
    earlier = jnp.dot(match, tri, preferred_element_type=jnp.float32).astype(jnp.int32)
    slot = jnp.where(match > 0, earlier, -1)
    slot_ref[...] = slot
    slots = lax.broadcasted_iota(jnp.int32, (cap, rows), 0)
    for k in range(2):
        onehot = (slot[k : k + 1, :] == slots).astype(jnp.bfloat16)
        picked = jnp.dot(onehot, tok_ref[...], preferred_element_type=jnp.float32)
        out_ref[k * cap : (k + 1) * cap, :] = picked.astype(jnp.bfloat16)


def dispatch(core, ids, tokens):
    rows, width = tokens.shape
    vmem = pl.BlockSpec(memory_space=pltpu.VMEM)
    return pl.pallas_call(
        dispatch_kernel,
        in_specs=[pl.BlockSpec(memory_space=pltpu.SMEM), vmem, vmem],
        out_specs=[vmem, vmem],
        out_shape=[
            jax.ShapeDtypeStruct((rows, width), jnp.bfloat16),
            jax.ShapeDtypeStruct((16, rows), jnp.int32),
        ],
        compiler_params=pltpu.CompilerParams(vmem_limit_bytes=VMEM_LIMIT),
        name="dispatch",
    )(core, ids, tokens)


def weigh_kernel(core_ref, ids_ref, gates_ref, slot_ref, pick_ref, weight_ref):
    rows = pick_ref.shape[0]
    cap = pick_ref.shape[1] // 2
    core = core_ref[0]
    kind = lax.broadcasted_iota(jnp.int32, (128, rows), 0)
    wanted = jnp.where(kind == 0, core, jnp.where(kind == 1, 1 - core, -1))
    weight = jnp.where(ids_ref[0:1, :] == wanted, gates_ref[0:1, :], 0.0)
    weight += jnp.where(ids_ref[1:2, :] == wanted, gates_ref[1:2, :], 0.0)
    weight_ref[...] = weight.T
    slot = jnp.where(kind == 0, slot_ref[0:1, :], slot_ref[1:2, :]).astype(jnp.float32).T
    slots = lax.broadcasted_iota(jnp.int32, (rows, cap), 1).astype(jnp.float32)
    for k in range(2):
        pick_ref[:, k * cap : (k + 1) * cap] = (slot[:, k : k + 1] == slots).astype(jnp.bfloat16)


def weigh(core, ids, gates, slot):
    rows = ids.shape[1]
    vmem = pl.BlockSpec(memory_space=pltpu.VMEM)
    return pl.pallas_call(
        weigh_kernel,
        in_specs=[pl.BlockSpec(memory_space=pltpu.SMEM)] + [vmem] * 3,
        out_specs=[vmem, vmem],
        out_shape=[
            jax.ShapeDtypeStruct((rows, rows), jnp.bfloat16),
            jax.ShapeDtypeStruct((rows, 128), jnp.float32),
        ],
        cost_estimate=pl.CostEstimate(flops=1 << 30, bytes_accessed=1 << 16, transcendentals=0),
        compiler_params=pltpu.CompilerParams(vmem_limit_bytes=VMEM_LIMIT),
        name="weigh",
    )(core, ids, gates, slot)


def combine_kernel(pick_ref, weight_ref, own_ref, back_ref, na_ref, nb_ref, nc_ref, out_ref):
    cap = own_ref.shape[1]
    total = jnp.zeros(out_ref.shape, jnp.float32)
    for k, first in enumerate((own_ref, back_ref)):
        at = slice(k * cap, (k + 1) * cap)
        done = first[0].astype(jnp.float32)
        for ref in (na_ref, nb_ref, nc_ref):
            done += ref[at, :].astype(jnp.float32)
        row = jnp.dot(pick_ref[:, at], done.astype(jnp.bfloat16), preferred_element_type=jnp.float32)
        total += weight_ref[:, k : k + 1] * row
    out_ref[...] = total.astype(jnp.bfloat16)


def combine(pick, weight, own, back, near):
    vmem = pl.BlockSpec(memory_space=pltpu.VMEM)
    return pl.pallas_call(
        combine_kernel,
        in_specs=[vmem] * 7,
        out_specs=vmem,
        out_shape=jax.ShapeDtypeStruct((pick.shape[0], own.shape[2]), jnp.bfloat16),
        compiler_params=pltpu.CompilerParams(vmem_limit_bytes=VMEM_LIMIT),
        name="combine",
    )(pick, weight, own, back, *near)


def load_kernel(here_ref, *refs):
    sources, targets, sem = refs[:3], refs[3:6], refs[6]
    copies = [pltpu.make_async_copy(a, b, sem.at[i]) for i, (a, b) in enumerate(zip(sources, targets))]
    for copy in copies:
        copy.start()
    for copy in copies:
        copy.wait()


def load(here, *weights):
    vmem = pl.BlockSpec(memory_space=pltpu.VMEM)
    hbm = pl.BlockSpec(memory_space=pl.ANY)
    return pl.pallas_call(
        load_kernel,
        in_specs=[pl.BlockSpec(memory_space=pltpu.SMEM)] + [hbm] * 3,
        out_specs=[vmem] * 3,
        out_shape=[jax.ShapeDtypeStruct(w.shape, w.dtype) for w in weights],
        scratch_shapes=[pltpu.SemaphoreType.DMA((3,))],
        compiler_params=pltpu.CompilerParams(vmem_limit_bytes=LOAD_VMEM),
        cost_estimate=pl.CostEstimate(flops=LOAD, bytes_accessed=1 << 16, transcendentals=0),
        name="load",
    )(here, *weights)


def add_blocks(chain, here_ref, pieces, wg, wu, acc_g=None, acc_u=None):
    core, me = here_ref[0], here_ref[1]
    rows, width = pieces[0][1].shape[1:]
    tile = wg.shape[1] // 2
    for n in range(2):
        cols = slice(n * tile, (n + 1) * tile)
        sums = []
        for acc, w in ((acc_g, wg), (acc_u, wu)):
            total = jnp.zeros((rows, tile), jnp.float32) if acc is None else acc[:, cols]
            for first, ref in pieces:
                for k in range(ref.shape[0]):
                    start = pl.multiple_of(block_of(core, me, chain, first + k) * width, width)
                    total += jnp.dot(ref[k], w[pl.ds(start, width), cols], preferred_element_type=jnp.float32)
            sums.append(total)
        yield cols, *sums


def early_kernel(chain, here_ref, held, third, fourth, wg, wu, acc_g, acc_u):
    for cols, g, u in add_blocks(chain, here_ref, [(0, held), (4, third), (8, fourth)], wg, wu):
        acc_g[:, cols] = g
        acc_u[:, cols] = u


def down_blocks(chain, here_ref, gated, wd, first, out):
    core, me = here_ref[0], here_ref[1]
    count, rows, width = out.shape
    for k in range(count):
        start = pl.multiple_of(block_of(core, me, chain, first + k) * width, width)
        y = jnp.dot(gated[...], wd[:, pl.ds(start, width)], preferred_element_type=jnp.float32)
        out[k] = y.astype(out.dtype)


def middle_kernel(chain, here_ref, last, acc_g, acc_u, wg, wu, wd, gated, send):
    for cols, g, u in add_blocks(chain, here_ref, [(12, last)], wg, wu, acc_g, acc_u):
        gated[:, cols] = (g / (1.0 + jnp.exp(-g)) * u).astype(jnp.bfloat16)
    down_blocks(chain, here_ref, gated, wd, 12, send)


def late_kernel(chain, here_ref, gated, wd, send, keep, rest):
    down_blocks(chain, here_ref, gated, wd, 8, send)
    down_blocks(chain, here_ref, gated, wd, 4, keep)
    down_blocks(chain, here_ref, gated, wd, 0, rest)


def local_kernel(kernel, name, cost, chain, outs, here, *operands):
    vmem = pl.BlockSpec(memory_space=pltpu.VMEM)
    return pl.pallas_call(
        functools.partial(kernel, chain),
        in_specs=[pl.BlockSpec(memory_space=pltpu.SMEM)] + [vmem] * len(operands),
        out_specs=[vmem] * len(outs),
        out_shape=[jax.ShapeDtypeStruct(shape, dtype) for shape, dtype in outs],
        compiler_params=pltpu.CompilerParams(vmem_limit_bytes=VMEM_LIMIT),
        cost_estimate=pl.CostEstimate(flops=cost, bytes_accessed=1 << 16, transcendentals=0),
        name=name,
    )(here, *operands)


def body(tokens, route_ids, route_gates, w_gate, w_up, w_down):
    rows, width = tokens.shape
    cap = rows // 2
    part = cap // 2
    hidden = w_gate.shape[2]
    wg, wu, wd = w_gate[0], w_up[0], w_down[0]
    core = lax.axis_index("expert").astype(jnp.int32).reshape(1)
    here = jnp.stack([lax.axis_index("expert"), lax.axis_index("tensor")]).astype(jnp.int32)
    both = range(2)

    bf16, f32 = jnp.bfloat16, jnp.float32
    block, square = (4, cap, width), (cap, hidden)

    ids, gates = route_ids.T, route_gates.T
    mine, slot = dispatch(core, ids, tokens)
    near = together([exchange(mine, 0, bits) for bits in (1, 2, 3)])
    own, oth = [jnp.stack([x[i * cap : (i + 1) * cap] for x in (mine, *near)]) for i in both]
    own, oth = together((own, oth))
    held = [own, lax.ppermute(oth, "expert", SWAP)]
    third = together([exchange(x, i, 4) for i, x in enumerate(held)])
    held, there, slot = together((held, here, slot))
    wg, wu, wd = load(there, wg, wu, wd)
    held, wd = together((held, wd))
    fourth = [exchange(x, i, 8) for i, x in enumerate(held)]
    last = [exchange(x, i, 8) for i, x in enumerate(third)]
    pick, weight = weigh(core, ids, gates, slot)

    third, pick, weight = together((third, pick, weight))
    early, token = [], ()
    for i in both:
        pieces, token = together(((held[i], third[i], fourth[i]), token))
        token = local_kernel(early_kernel, "early", EARLY[i], i, [(square, f32)] * 2, here, *pieces, wg, wu)
        early.append(token)
    middle, later = [], []
    for i in both:
        arrived, sums, token = together((last[i], early[i], token))
        token = local_kernel(
            middle_kernel, "middle", MIDDLE, i, [(square, bf16), (block, bf16)], here, arrived, *sums, wg, wu, wd
        )
        middle.append(token)
    for i in both:
        gated, token = together((middle[i][0], token))
        token = local_kernel(late_kernel, "late", LATE, i, [(block, bf16)] + [(block, f32)] * 2, here, gated, wd)
        later.append(token)

    (send, keep, rest), other = later
    keep, other = together((keep, other))
    later = [(send, keep, rest), other]
    total = []
    for i in both:
        send, keep, rest = later[i]
        gone = exchange(middle[i][1], i, 8)
        also = exchange(send, i, 8)
        second = exchange((keep + gone.astype(f32)).astype(bf16), i, 4)
        total.append(rest + also.astype(f32) + second.astype(f32))
    own, oth = together(total)
    back = lax.ppermute(oth.astype(bf16), "expert", SWAP)
    own, back = together((own, back))
    send = [jnp.concatenate([own[bits].astype(bf16), back[bits]]) for bits in (1, 2, 3)]
    send = together(send)
    near = together([exchange(x, 0, bits) for bits, x in zip((1, 2, 3), send)])
    return combine(pick, weight, own[:1], back[:1], near)


def solution(mesh):
    placed = (
        P(("dp", "expert"), "tensor"),
        P(("dp", "expert"), None),
        P(("dp", "expert"), None),
        P("expert", None, "tensor"),
        P("expert", None, "tensor"),
        P("expert", "tensor", None),
    )
    return jax.shard_map(
        body, mesh=mesh, in_specs=placed, out_specs=P(("dp", "expert"), "tensor"), check_vma=False
    )
```

```python
import functools

import jax
import jax.numpy as jnp
from jax import lax
from jax.experimental import pallas as pl
from jax.experimental.pallas import tpu as pltpu
from jax.sharding import PartitionSpec as P

TENSOR = 16
MASKS = (1, 3, 4, 12)
VMEM_LIMIT = 8 << 20
LOAD_VMEM = 32 << 20
LOAD, EARLY, MIDDLE, LATE = 1 << 33, (1 << 32, 1 << 20), 1 << 32, 1 << 20


CHAINS = (((0, 2, 1, 3), (1, 3, 0, 2)), ((1, 3, 2, 0), (0, 2, 3, 1)))
SWAP = [(0, 1), (1, 0)]


def mask_of(core, chain, bits):
    mask = 0
    for phase in range(4):
        if bits >> phase & 1:
            mask ^= MASKS[CHAINS[core][chain][phase]]
    return mask


def block_of(core, me, chain, bits):
    return me ^ jnp.where(core == 0, mask_of(0, chain, bits), mask_of(1, chain, bits))


def exchange(value, chain, bits, cross=False):
    pairs = []
    for core in range(2):
        mask = mask_of(core, chain, bits)
        target = 1 - core if cross else core
        pairs += [(core * TENSOR + t, target * TENSOR + (t ^ mask)) for t in range(TENSOR)]
    return lax.ppermute(value, ("expert", "tensor"), pairs)


together = lax.optimization_barrier


def exchange_pair(values, bits, cross=False):
    values = together(list(values))
    return together([exchange(values[i], i, bits, cross and i == 1) for i in range(2)])


def dispatch_kernel(core_ref, ids_ref, tok_ref, out_ref, slot_ref):
    rows = tok_ref.shape[0]
    cap = out_ref.shape[0] // 2
    core = core_ref[0]
    kinds = slot_ref.shape[0]
    tri = (
        lax.broadcasted_iota(jnp.int32, (rows, rows), 0) < lax.broadcasted_iota(jnp.int32, (rows, rows), 1)
    ).astype(jnp.bfloat16)
    kind = lax.broadcasted_iota(jnp.int32, (kinds, rows), 0)
    wanted = jnp.where(kind == 0, core, jnp.where(kind == 1, 1 - core, -1))
    match = ((ids_ref[0:1, :] == wanted) | (ids_ref[1:2, :] == wanted)).astype(jnp.bfloat16)
    earlier = jnp.dot(match, tri, preferred_element_type=jnp.float32).astype(jnp.int32)
    slot = jnp.where(match > 0, earlier, -1)
    slot_ref[...] = slot
    slots = lax.broadcasted_iota(jnp.int32, (cap, rows), 0)
    for k in range(2):
        onehot = (slot[k : k + 1, :] == slots).astype(jnp.bfloat16)
        picked = jnp.dot(onehot, tok_ref[...], preferred_element_type=jnp.float32)
        out_ref[k * cap : (k + 1) * cap, :] = picked.astype(jnp.bfloat16)


def dispatch(core, ids, tokens):
    rows, width = tokens.shape
    vmem = pl.BlockSpec(memory_space=pltpu.VMEM)
    return pl.pallas_call(
        dispatch_kernel,
        in_specs=[pl.BlockSpec(memory_space=pltpu.SMEM), vmem, vmem],
        out_specs=[vmem, vmem],
        out_shape=[
            jax.ShapeDtypeStruct((rows, width), jnp.bfloat16),
            jax.ShapeDtypeStruct((16, rows), jnp.int32),
        ],
        compiler_params=pltpu.CompilerParams(vmem_limit_bytes=VMEM_LIMIT),
        name="dispatch",
    )(core, ids, tokens)


def weigh_kernel(core_ref, ids_ref, gates_ref, slot_ref, pick_ref, weight_ref):
    rows = pick_ref.shape[0]
    cap = pick_ref.shape[1] // 2
    core = core_ref[0]
    kind = lax.broadcasted_iota(jnp.int32, (128, rows), 0)
    wanted = jnp.where(kind == 0, core, jnp.where(kind == 1, 1 - core, -1))
    weight = jnp.where(ids_ref[0:1, :] == wanted, gates_ref[0:1, :], 0.0)
    weight += jnp.where(ids_ref[1:2, :] == wanted, gates_ref[1:2, :], 0.0)
    weight_ref[...] = weight.T
    slot = jnp.where(kind == 0, slot_ref[0:1, :], slot_ref[1:2, :]).astype(jnp.float32).T
    slots = lax.broadcasted_iota(jnp.int32, (rows, cap), 1).astype(jnp.float32)
    for k in range(2):
        pick_ref[:, k * cap : (k + 1) * cap] = (slot[:, k : k + 1] == slots).astype(jnp.bfloat16)


def weigh(core, ids, gates, slot):
    rows = ids.shape[1]
    vmem = pl.BlockSpec(memory_space=pltpu.VMEM)
    return pl.pallas_call(
        weigh_kernel,
        in_specs=[pl.BlockSpec(memory_space=pltpu.SMEM)] + [vmem] * 3,
        out_specs=[vmem, vmem],
        out_shape=[
            jax.ShapeDtypeStruct((rows, rows), jnp.bfloat16),
            jax.ShapeDtypeStruct((rows, 128), jnp.float32),
        ],
        cost_estimate=pl.CostEstimate(flops=1 << 30, bytes_accessed=1 << 16, transcendentals=0),
        compiler_params=pltpu.CompilerParams(vmem_limit_bytes=VMEM_LIMIT),
        name="weigh",
    )(core, ids, gates, slot)


def combine_kernel(pick_ref, weight_ref, own_ref, back_ref, na_ref, nb_ref, nc_ref, out_ref):
    cap = own_ref.shape[1]
    total = jnp.zeros(out_ref.shape, jnp.float32)
    for k, first in enumerate((own_ref, back_ref)):
        at = slice(k * cap, (k + 1) * cap)
        done = first[0].astype(jnp.float32)
        for ref in (na_ref, nb_ref, nc_ref):
            done += ref[at, :].astype(jnp.float32)
        row = jnp.dot(pick_ref[:, at], done.astype(jnp.bfloat16), preferred_element_type=jnp.float32)
        total += weight_ref[:, k : k + 1] * row
    out_ref[...] = total.astype(jnp.bfloat16)


def combine(pick, weight, own, back, near):
    vmem = pl.BlockSpec(memory_space=pltpu.VMEM)
    return pl.pallas_call(
        combine_kernel,
        in_specs=[vmem] * 7,
        out_specs=vmem,
        out_shape=jax.ShapeDtypeStruct((pick.shape[0], own.shape[2]), jnp.bfloat16),
        compiler_params=pltpu.CompilerParams(vmem_limit_bytes=VMEM_LIMIT),
        name="combine",
    )(pick, weight, own, back, *near)


def load_kernel(here_ref, *refs):
    sources, targets, sem = refs[:3], refs[3:6], refs[6]
    copies = [pltpu.make_async_copy(a, b, sem.at[i]) for i, (a, b) in enumerate(zip(sources, targets))]
    for copy in copies:
        copy.start()
    for copy in copies:
        copy.wait()


def load(here, *weights):
    vmem = pl.BlockSpec(memory_space=pltpu.VMEM)
    hbm = pl.BlockSpec(memory_space=pl.ANY)
    return pl.pallas_call(
        load_kernel,
        in_specs=[pl.BlockSpec(memory_space=pltpu.SMEM)] + [hbm] * 3,
        out_specs=[vmem] * 3,
        out_shape=[jax.ShapeDtypeStruct(w.shape, w.dtype) for w in weights],
        scratch_shapes=[pltpu.SemaphoreType.DMA((3,))],
        compiler_params=pltpu.CompilerParams(vmem_limit_bytes=LOAD_VMEM),
        cost_estimate=pl.CostEstimate(flops=LOAD, bytes_accessed=1 << 16, transcendentals=0),
        name="load",
    )(here, *weights)


def add_blocks(chain, here_ref, pieces, wg, wu, acc_g=None, acc_u=None):
    core, me = here_ref[0], here_ref[1]
    rows, width = pieces[0][1].shape[1:]
    tile = wg.shape[1] // 2
    for n in range(2):
        cols = slice(n * tile, (n + 1) * tile)
        sums = []
        for acc, w in ((acc_g, wg), (acc_u, wu)):
            total = jnp.zeros((rows, tile), jnp.float32) if acc is None else acc[:, cols]
            for first, ref in pieces:
                for k in range(ref.shape[0]):
                    start = pl.multiple_of(block_of(core, me, chain, first + k) * width, width)
                    total += jnp.dot(ref[k], w[pl.ds(start, width), cols], preferred_element_type=jnp.float32)
            sums.append(total)
        yield cols, *sums


def early_kernel(chain, here_ref, held, third, fourth, wg, wu, acc_g, acc_u):
    for cols, g, u in add_blocks(chain, here_ref, [(0, held), (4, third), (8, fourth)], wg, wu):
        acc_g[:, cols] = g
        acc_u[:, cols] = u


def down_blocks(chain, here_ref, gated, wd, first, out):
    core, me = here_ref[0], here_ref[1]
    count, rows, width = out.shape
    for k in range(count):
        start = pl.multiple_of(block_of(core, me, chain, first + k) * width, width)
        y = jnp.dot(gated[...], wd[:, pl.ds(start, width)], preferred_element_type=jnp.float32)
        out[k] = y.astype(out.dtype)


def middle_kernel(here_ref, la, lb, ga, ua, gb, ub, wg, wu, wd, gated_a, gated_b, send_a, send_b):
    chains = ((la, ga, ua, gated_a, send_a), (lb, gb, ub, gated_b, send_b))
    for chain, (last, acc_g, acc_u, gated, send) in enumerate(chains):
        for cols, g, u in add_blocks(chain, here_ref, [(12, last)], wg, wu, acc_g, acc_u):
            gated[:, cols] = (g / (1.0 + jnp.exp(-g)) * u).astype(jnp.bfloat16)
        down_blocks(chain, here_ref, gated, wd, 12, send)


def late_kernel(here_ref, gated_a, gated_b, wd, send_a, send_b, keep_a, keep_b, rest_a, rest_b):
    for first, outs in ((8, (send_a, send_b)), (4, (keep_a, keep_b)), (0, (rest_a, rest_b))):
        for chain, gated in enumerate((gated_a, gated_b)):
            down_blocks(chain, here_ref, gated, wd, first, outs[chain])


def local_kernel(kernel, name, cost, outs, here, *operands):
    vmem = pl.BlockSpec(memory_space=pltpu.VMEM)
    return pl.pallas_call(
        kernel,
        in_specs=[pl.BlockSpec(memory_space=pltpu.SMEM)] + [vmem] * len(operands),
        out_specs=[vmem] * len(outs),
        out_shape=[jax.ShapeDtypeStruct(shape, dtype) for shape, dtype in outs],
        compiler_params=pltpu.CompilerParams(vmem_limit_bytes=VMEM_LIMIT),
        cost_estimate=pl.CostEstimate(flops=cost, bytes_accessed=1 << 16, transcendentals=0),
        name=name,
    )(here, *operands)


def body(tokens, route_ids, route_gates, w_gate, w_up, w_down):
    rows, width = tokens.shape
    cap = rows // 2
    part = cap // 2
    hidden = w_gate.shape[2]
    wg, wu, wd = w_gate[0], w_up[0], w_down[0]
    core = lax.axis_index("expert").astype(jnp.int32).reshape(1)
    here = jnp.stack([lax.axis_index("expert"), lax.axis_index("tensor")]).astype(jnp.int32)
    both = range(2)

    bf16, f32 = jnp.bfloat16, jnp.float32
    block, square = (4, cap, width), (cap, hidden)

    ids, gates = route_ids.T, route_gates.T
    mine, slot = dispatch(core, ids, tokens)
    near = together([exchange(mine, 0, bits) for bits in (1, 2, 3)])
    own, oth = [jnp.stack([x[i * cap : (i + 1) * cap] for x in (mine, *near)]) for i in both]
    own, oth = together((own, oth))
    held = [own, lax.ppermute(oth, "expert", SWAP)]
    third = together([exchange(x, i, 4) for i, x in enumerate(held)])
    held, there, slot = together((held, here, slot))
    wg, wu, wd = load(there, wg, wu, wd)
    held, wd = together((held, wd))
    fourth = [exchange(x, i, 8) for i, x in enumerate(held)]
    last = [exchange(x, i, 8) for i, x in enumerate(third)]
    pick, weight = weigh(core, ids, gates, slot)

    third, pick, weight = together((third, pick, weight))
    early, token = [], ()
    for i in both:
        pieces, token = together(((held[i], third[i], fourth[i]), token))
        token = local_kernel(
            functools.partial(early_kernel, i), "early", EARLY[i], [(square, f32)] * 2, here, *pieces, wg, wu
        )
        early.append(token)
    last = together(last)
    *gated, send_a, send_b = local_kernel(
        middle_kernel, "middle", MIDDLE, [(square, bf16)] * 2 + [(block, bf16)] * 2, here, *last, *early[0], *early[1], wg, wu, wd
    )
    gone = exchange_pair([send_a, send_b], 8)
    out = local_kernel(late_kernel, "late", LATE, [(block, bf16)] * 2 + [(block, f32)] * 4, here, *gated, wd)
    also = exchange_pair(out[0:2], 8)
    second = exchange_pair([(out[2 + i] + gone[i].astype(f32)).astype(bf16) for i in both], 4, cross=True)
    own, oth = [out[4 + i] + also[i].astype(f32) for i in both]
    back = lax.ppermute(oth.astype(bf16), "expert", SWAP)
    own, back = together((own + second[0].astype(f32), (back.astype(f32) + second[1].astype(f32)).astype(bf16)))
    send = [jnp.concatenate([own[bits].astype(bf16), back[bits]]) for bits in (1, 2, 3)]
    send = together(send)
    near = together([exchange(x, 0, bits) for bits, x in zip((1, 2, 3), send)])
    return combine(pick, weight, own[:1], back[:1], near)


def solution(mesh):
    placed = (
        P(("dp", "expert"), "tensor"),
        P(("dp", "expert"), None),
        P(("dp", "expert"), None),
        P("expert", None, "tensor"),
        P("expert", None, "tensor"),
        P("expert", "tensor", None),
    )
    return jax.shard_map(
        body, mesh=mesh, in_specs=placed, out_specs=P(("dp", "expert"), "tensor"), check_vma=False
    )
```

```python
import functools

import jax
import jax.numpy as jnp
from jax import lax
from jax.experimental import pallas as pl
from jax.experimental.pallas import tpu as pltpu
from jax.sharding import PartitionSpec as P

TENSOR = 16
MASKS = (1, 3, 4, 12)
VMEM_LIMIT = 8 << 20
LOAD_VMEM = 32 << 20
LOAD, EARLY, MIDDLE, LATE = 1 << 33, (1 << 32, 1 << 20), 1 << 32, 1 << 20


CHAINS = (((0, 2, 1, 3), (1, 3, 0, 2)), ((1, 3, 2, 0), (0, 2, 3, 1)))
SWAP = [(0, 1), (1, 0)]


def mask_of(core, chain, bits):
    mask = 0
    for phase in range(4):
        if bits >> phase & 1:
            mask ^= MASKS[CHAINS[core][chain][phase]]
    return mask


def block_of(core, me, chain, bits):
    return me ^ jnp.where(core == 0, mask_of(0, chain, bits), mask_of(1, chain, bits))


def exchange(value, chain, bits, cross=False):
    pairs = []
    for core in range(2):
        mask = mask_of(core, chain, bits)
        target = 1 - core if cross else core
        pairs += [(core * TENSOR + t, target * TENSOR + (t ^ mask)) for t in range(TENSOR)]
    return lax.ppermute(value, ("expert", "tensor"), pairs)


together = lax.optimization_barrier


def exchange_pair(values, bits, cross=False):
    values = together(list(values))
    return together([exchange(values[i], i, bits, cross and i == 1) for i in range(2)])


def dispatch_kernel(core_ref, ids_hbm, tok_hbm, out_ref, slot_ref, ids_ref, tok_ref, sem):
    ids_copy = pltpu.make_async_copy(ids_hbm, ids_ref, sem.at[0])
    tok_copy = pltpu.make_async_copy(tok_hbm, tok_ref, sem.at[1])
    ids_copy.start()
    tok_copy.start()
    rows = tok_ref.shape[0]
    cap = out_ref.shape[0] // 2
    core = core_ref[0]
    kinds = slot_ref.shape[0]
    tri = (
        lax.broadcasted_iota(jnp.int32, (rows, rows), 0) < lax.broadcasted_iota(jnp.int32, (rows, rows), 1)
    ).astype(jnp.bfloat16)
    kind = lax.broadcasted_iota(jnp.int32, (kinds, rows), 0)
    wanted = jnp.where(kind == 0, core, jnp.where(kind == 1, 1 - core, -1))
    ids_copy.wait()
    match = ((ids_ref[0:1, :] == wanted) | (ids_ref[1:2, :] == wanted)).astype(jnp.bfloat16)
    earlier = jnp.dot(match, tri, preferred_element_type=jnp.float32).astype(jnp.int32)
    slot = jnp.where(match > 0, earlier, -1)
    slot_ref[...] = slot
    slots = lax.broadcasted_iota(jnp.int32, (cap, rows), 0)
    tok_copy.wait()
    for k in range(2):
        onehot = (slot[k : k + 1, :] == slots).astype(jnp.bfloat16)
        picked = jnp.dot(onehot, tok_ref[...], preferred_element_type=jnp.float32)
        out_ref[k * cap : (k + 1) * cap, :] = picked.astype(jnp.bfloat16)


def dispatch(core, ids, tokens):
    rows, width = tokens.shape
    vmem = pl.BlockSpec(memory_space=pltpu.VMEM)
    hbm = pl.BlockSpec(memory_space=pl.ANY)
    return pl.pallas_call(
        dispatch_kernel,
        in_specs=[pl.BlockSpec(memory_space=pltpu.SMEM), hbm, hbm],
        out_specs=[vmem, vmem],
        out_shape=[
            jax.ShapeDtypeStruct((rows, width), jnp.bfloat16),
            jax.ShapeDtypeStruct((16, rows), jnp.int32),
        ],
        scratch_shapes=[
            pltpu.VMEM(ids.shape, ids.dtype),
            pltpu.VMEM(tokens.shape, tokens.dtype),
            pltpu.SemaphoreType.DMA((2,)),
        ],
        name="dispatch",
    )(core, ids, tokens)


def weigh_kernel(core_ref, ids_ref, gates_ref, slot_ref, pick_ref, weight_ref):
    rows = pick_ref.shape[0]
    cap = pick_ref.shape[1] // 2
    core = core_ref[0]
    kind = lax.broadcasted_iota(jnp.int32, (128, rows), 0)
    wanted = jnp.where(kind == 0, core, jnp.where(kind == 1, 1 - core, -1))
    weight = jnp.where(ids_ref[0:1, :] == wanted, gates_ref[0:1, :], 0.0)
    weight += jnp.where(ids_ref[1:2, :] == wanted, gates_ref[1:2, :], 0.0)
    weight_ref[...] = weight.T
    slot = jnp.where(kind == 0, slot_ref[0:1, :], slot_ref[1:2, :]).astype(jnp.float32).T
    slots = lax.broadcasted_iota(jnp.int32, (rows, cap), 1).astype(jnp.float32)
    for k in range(2):
        pick_ref[:, k * cap : (k + 1) * cap] = (slot[:, k : k + 1] == slots).astype(jnp.bfloat16)


def weigh(core, ids, gates, slot):
    rows = ids.shape[1]
    vmem = pl.BlockSpec(memory_space=pltpu.VMEM)
    return pl.pallas_call(
        weigh_kernel,
        in_specs=[pl.BlockSpec(memory_space=pltpu.SMEM)] + [vmem] * 3,
        out_specs=[vmem, vmem],
        out_shape=[
            jax.ShapeDtypeStruct((rows, rows), jnp.bfloat16),
            jax.ShapeDtypeStruct((rows, 128), jnp.float32),
        ],
        cost_estimate=pl.CostEstimate(flops=1 << 30, bytes_accessed=1 << 16, transcendentals=0),
        compiler_params=pltpu.CompilerParams(vmem_limit_bytes=VMEM_LIMIT),
        name="weigh",
    )(core, ids, gates, slot)


def combine_kernel(pick_ref, weight_ref, own_ref, back_ref, na_ref, nb_ref, nc_ref, out_ref):
    cap = own_ref.shape[1]
    total = jnp.zeros(out_ref.shape, jnp.float32)
    for k, first in enumerate((own_ref, back_ref)):
        at = slice(k * cap, (k + 1) * cap)
        done = first[0].astype(jnp.float32)
        for ref in (na_ref, nb_ref, nc_ref):
            done += ref[at, :].astype(jnp.float32)
        row = jnp.dot(pick_ref[:, at], done.astype(jnp.bfloat16), preferred_element_type=jnp.float32)
        total += weight_ref[:, k : k + 1] * row
    out_ref[...] = total.astype(jnp.bfloat16)


def combine(pick, weight, own, back, near):
    vmem = pl.BlockSpec(memory_space=pltpu.VMEM)
    return pl.pallas_call(
        combine_kernel,
        in_specs=[vmem] * 7,
        out_specs=vmem,
        out_shape=jax.ShapeDtypeStruct((pick.shape[0], own.shape[2]), jnp.bfloat16),
        compiler_params=pltpu.CompilerParams(vmem_limit_bytes=VMEM_LIMIT),
        name="combine",
    )(pick, weight, own, back, *near)


def load_kernel(here_ref, *refs):
    sources, targets, sem = refs[:3], refs[3:6], refs[6]
    copies = [pltpu.make_async_copy(a, b, sem.at[i]) for i, (a, b) in enumerate(zip(sources, targets))]
    for copy in copies:
        copy.start()
    for copy in copies:
        copy.wait()


def load(here, *weights):
    vmem = pl.BlockSpec(memory_space=pltpu.VMEM)
    hbm = pl.BlockSpec(memory_space=pl.ANY)
    return pl.pallas_call(
        load_kernel,
        in_specs=[pl.BlockSpec(memory_space=pltpu.SMEM)] + [hbm] * 3,
        out_specs=[vmem] * 3,
        out_shape=[jax.ShapeDtypeStruct(w.shape, w.dtype) for w in weights],
        scratch_shapes=[pltpu.SemaphoreType.DMA((3,))],
        compiler_params=pltpu.CompilerParams(vmem_limit_bytes=LOAD_VMEM),
        cost_estimate=pl.CostEstimate(flops=LOAD, bytes_accessed=1 << 16, transcendentals=0),
        name="load",
    )(here, *weights)


def add_blocks(chain, here_ref, pieces, wg, wu, acc_g=None, acc_u=None):
    core, me = here_ref[0], here_ref[1]
    rows, width = pieces[0][1].shape[1:]
    tile = wg.shape[1] // 2
    for n in range(2):
        cols = slice(n * tile, (n + 1) * tile)
        sums = []
        for acc, w in ((acc_g, wg), (acc_u, wu)):
            total = jnp.zeros((rows, tile), jnp.float32) if acc is None else acc[:, cols]
            for first, ref in pieces:
                for k in range(ref.shape[0]):
                    start = pl.multiple_of(block_of(core, me, chain, first + k) * width, width)
                    total += jnp.dot(ref[k], w[pl.ds(start, width), cols], preferred_element_type=jnp.float32)
            sums.append(total)
        yield cols, *sums


def early_kernel(chain, here_ref, held, third, fourth, wg, wu, acc_g, acc_u):
    for cols, g, u in add_blocks(chain, here_ref, [(0, held), (4, third), (8, fourth)], wg, wu):
        acc_g[:, cols] = g
        acc_u[:, cols] = u


def down_blocks(chain, here_ref, gated, wd, first, out):
    core, me = here_ref[0], here_ref[1]
    count, rows, width = out.shape
    for k in range(count):
        start = pl.multiple_of(block_of(core, me, chain, first + k) * width, width)
        y = jnp.dot(gated[...], wd[:, pl.ds(start, width)], preferred_element_type=jnp.float32)
        out[k] = y.astype(out.dtype)


def middle_kernel(here_ref, la, lb, ga, ua, gb, ub, wg, wu, wd, gated_a, gated_b, send_a, send_b):
    chains = ((la, ga, ua, gated_a, send_a), (lb, gb, ub, gated_b, send_b))
    for chain, (last, acc_g, acc_u, gated, send) in enumerate(chains):
        for cols, g, u in add_blocks(chain, here_ref, [(12, last)], wg, wu, acc_g, acc_u):
            gated[:, cols] = (g / (1.0 + jnp.exp(-g)) * u).astype(jnp.bfloat16)
        down_blocks(chain, here_ref, gated, wd, 12, send)


def late_kernel(here_ref, gated_a, gated_b, wd, send_a, send_b, keep_a, keep_b, rest_a, rest_b):
    for first, outs in ((8, (send_a, send_b)), (4, (keep_a, keep_b)), (0, (rest_a, rest_b))):
        for chain, gated in enumerate((gated_a, gated_b)):
            down_blocks(chain, here_ref, gated, wd, first, outs[chain])


def local_kernel(kernel, name, cost, outs, here, *operands):
    vmem = pl.BlockSpec(memory_space=pltpu.VMEM)
    return pl.pallas_call(
        kernel,
        in_specs=[pl.BlockSpec(memory_space=pltpu.SMEM)] + [vmem] * len(operands),
        out_specs=[vmem] * len(outs),
        out_shape=[jax.ShapeDtypeStruct(shape, dtype) for shape, dtype in outs],
        compiler_params=pltpu.CompilerParams(vmem_limit_bytes=VMEM_LIMIT),
        cost_estimate=pl.CostEstimate(flops=cost, bytes_accessed=1 << 16, transcendentals=0),
        name=name,
    )(here, *operands)


def body(tokens, route_ids, route_gates, w_gate, w_up, w_down):
    rows, width = tokens.shape
    cap = rows // 2
    part = cap // 2
    hidden = w_gate.shape[2]
    wg, wu, wd = w_gate[0], w_up[0], w_down[0]
    core = lax.axis_index("expert").astype(jnp.int32).reshape(1)
    here = jnp.stack([lax.axis_index("expert"), lax.axis_index("tensor")]).astype(jnp.int32)
    both = range(2)

    bf16, f32 = jnp.bfloat16, jnp.float32
    block, square = (4, cap, width), (cap, hidden)

    ids, gates = route_ids.T, route_gates.T
    mine, slot = dispatch(core, ids, tokens)
    near = together([exchange(mine, 0, bits) for bits in (1, 2, 3)])
    own, oth = [jnp.stack([x[i * cap : (i + 1) * cap] for x in (mine, *near)]) for i in both]
    own, oth = together((own, oth))
    held = [own, lax.ppermute(oth, "expert", SWAP)]
    third = together([exchange(x, i, 4) for i, x in enumerate(held)])
    held, there, slot = together((held, here, slot))
    wg, wu, wd = load(there, wg, wu, wd)
    held, wd = together((held, wd))
    fourth = [exchange(x, i, 8) for i, x in enumerate(held)]
    last = [exchange(x, i, 8) for i, x in enumerate(third)]
    pick, weight = weigh(core, ids, gates, slot)

    third, pick, weight = together((third, pick, weight))
    early, token = [], ()
    for i in both:
        pieces, token = together(((held[i], third[i], fourth[i]), token))
        token = local_kernel(
            functools.partial(early_kernel, i), "early", EARLY[i], [(square, f32)] * 2, here, *pieces, wg, wu
        )
        early.append(token)
    last = together(last)
    *gated, send_a, send_b = local_kernel(
        middle_kernel, "middle", MIDDLE, [(square, bf16)] * 2 + [(block, bf16)] * 2, here, *last, *early[0], *early[1], wg, wu, wd
    )
    gone = exchange_pair([send_a, send_b], 8)
    out = local_kernel(late_kernel, "late", LATE, [(block, bf16)] * 2 + [(block, f32)] * 4, here, *gated, wd)
    also = exchange_pair(out[0:2], 8)
    second = exchange_pair([(out[2 + i] + gone[i].astype(f32)).astype(bf16) for i in both], 4, cross=True)
    own, oth = [out[4 + i] + also[i].astype(f32) for i in both]
    back = lax.ppermute(oth.astype(bf16), "expert", SWAP)
    own, back = together((own + second[0].astype(f32), (back.astype(f32) + second[1].astype(f32)).astype(bf16)))
    send = [jnp.concatenate([own[bits].astype(bf16), back[bits]]) for bits in (1, 2, 3)]
    send = together(send)
    near = together([exchange(x, 0, bits) for bits, x in zip((1, 2, 3), send)])
    return combine(pick, weight, own[:1], back[:1], near)


def solution(mesh):
    placed = (
        P(("dp", "expert"), "tensor"),
        P(("dp", "expert"), None),
        P(("dp", "expert"), None),
        P("expert", None, "tensor"),
        P("expert", None, "tensor"),
        P("expert", "tensor", None),
    )
    return jax.shard_map(
        body, mesh=mesh, in_specs=placed, out_specs=P(("dp", "expert"), "tensor"), check_vma=False
    )
```
